32 devices in a mesh: section: 2 (over core), ctx: 16 (over z, y, x).
Axes of the slice: x: 2, y: 2, z: 4, core: 2. Of those that a mesh axis runs over, the one named last changes fastest.
Arguments:
- down_queries: bfloat16 [2, 2048, 2304], P('section', 'ctx'), may hold values from -40 to 40
- down_keys: bfloat16 [2, 2048, 2304], P('section', 'ctx'), may hold values from -40 to 40
- down_values: bfloat16 [2, 2048, 2304], P('section', 'ctx'), may hold values from -6 to 6
- up_queries: bfloat16 [2, 2048, 2304], P('section', 'ctx'), may hold values from -40 to 40
- up_keys: bfloat16 [2, 2048, 2304], P('section', 'ctx'), may hold values from -40 to 40
- up_values: bfloat16 [2, 2048, 2304], P('section', 'ctx'), may hold values from -6 to 6
- key_blocks: int32 [16, 2], P('ctx'), may hold values from -1 to 11, as said below
Outputs:
- forward: bfloat16 [2, 2048, 2304], P('section', 'ctx')
- handed: bfloat16 [2, 2048, 2304], P('section', 'ctx')
The draws below stay inside these ranges and needn't reach their ends.
Inputs may be any that keep to these rules, and one draw needn't show every extreme that they name: `key_blocks`: slot k (counting from 1) of query block i holds i - k * 4 or -1, and -1 wherever i - k * 4 is negative.
All inputs are finite; a program needn't handle non-finite values.
Results may differ from the reference program's by a relative error of at most 0.0038.
Values may be sent and summed in bfloat16 or wider, within the bound.
No kernel may reach another device: no remote copies, remote signals or barrier semaphores. Data moves between devices by JAX's collectives and lax.ppermute only.
A program may use at most 64 MiB of HBM per device.

```python
import math
import jax
import jax.numpy as jnp
from jax import lax

HEAD_DIM = 64
HEADS = 36
D = 2304
BLOCK = 128
NSTR = 2
TOKENS = 2048
NB = 16
STRIDE = 4
N_SECTION = 2


def draw_pair(key, salt):
    key = jax.random.fold_in(key, salt)
    subkeys = jax.random.split(key, 5)
    full_shape = (N_SECTION, TOKENS, D)
    query_scale = jnp.exp(jax.random.uniform(subkeys[3], (N_SECTION, TOKENS, 1), jnp.float32, 0.0, math.log(4.0)))
    key_scale = jnp.exp(jax.random.uniform(subkeys[4], (N_SECTION, TOKENS, 1), jnp.float32, 0.0, math.log(4.0)))
    query_rows = jax.random.normal(subkeys[0], full_shape, jnp.float32) * query_scale
    key_rows = jax.random.normal(subkeys[1], full_shape, jnp.float32) * key_scale
    return (jnp.clip(query_rows, -40.0, 40.0).astype(jnp.bfloat16), jnp.clip(key_rows, -40.0, 40.0).astype(jnp.bfloat16))


def draw_down_queries(key, part):
    return draw_pair(key, 11)[0]


def draw_down_keys(key, part):
    return draw_pair(key, 11)[1]


def draw_up_queries(key, part):
    return draw_pair(key, 23)[0]


def draw_up_keys(key, part):
    return draw_pair(key, 23)[1]


def draw_key_blocks(key, part):
    key = jax.random.fold_in(key, 41)
    block_ids = jnp.arange(NB, dtype=jnp.int32)[:, None]
    offset_steps = jnp.arange(1, NSTR + 1, dtype=jnp.int32)[None, :]
    target = block_ids - offset_steps * STRIDE
    keeping = jax.random.randint(key, (NB, NSTR), 0, 4) < 3
    keeping = keeping | (block_ids == NB - 1)
    return jnp.where((target >= 0) & keeping, target, -1).astype(jnp.int32)


def shard_levels(rng, shape, cuts, smallest, top_value):
    factor_of = 1.0
    for dim, parts in cuts:
        heights = jax.random.uniform(jax.random.fold_in(jax.random.fold_in(rng, 6), dim), (parts,), jnp.float32, smallest / len(cuts), top_value / len(cuts))
        factor_of = factor_of * jnp.repeat(jnp.exp(heights), shape[dim] // parts).reshape((-1,) + (1,) * (len(shape) - 1 - dim))
    return factor_of


def bell_draw(key, shape, spread, most, cuts=(), kind=jnp.bfloat16):
    result = jax.random.normal(key, shape, jnp.float32) * spread
    if len(cuts) > 0:
        result = shard_levels(key, shape, cuts, -0.22, 0.18) * result
    return jnp.clip(result, min=-most, max=most).astype(kind)


def setup_inputs(seed: int = 0) -> dict:
    seeds = jax.random.split(jax.random.key(seed), 8)
    return {
        "down_queries": draw_down_queries(jax.random.fold_in(seeds[7], 71), 0),
        "down_keys": draw_down_keys(jax.random.fold_in(seeds[7], 71), 0),
        "down_values": bell_draw(seeds[2], (N_SECTION, TOKENS, D), 1.0, 6.0, ((0, 2), (1, 16))),
        "up_queries": draw_up_queries(jax.random.fold_in(seeds[7], 71), 0),
        "up_keys": draw_up_keys(jax.random.fold_in(seeds[7], 71), 0),
        "up_values": bell_draw(seeds[5], (N_SECTION, TOKENS, D), 1.0, 6.0, ((0, 2), (1, 16))),
        "key_blocks": draw_key_blocks(jax.random.fold_in(seeds[7], 71), 0),
    }


def attention(query_in, key_in, value_in, key_blocks):
    queries = query_in.reshape(NB, BLOCK, HEADS, HEAD_DIM)
    key_rows = key_in.reshape(NB, BLOCK, HEADS, HEAD_DIM)
    value_rows = value_in.reshape(NB, BLOCK, HEADS, HEAD_DIM)
    causal = jnp.arange(BLOCK)[:, None] >= jnp.arange(BLOCK)[None, :]
    scale = 1.0 / math.sqrt(HEAD_DIM)

    def attend(block_index):
        listed = key_blocks[block_index]
        key_parts = [key_rows[block_index]]
        value_parts = [value_rows[block_index]]
        allowed = [causal]
        for offset_step in range(NSTR):
            source_block = jnp.maximum(listed[offset_step], 0).astype(jnp.int32)
            key_parts.append(key_rows[source_block])
            value_parts.append(value_rows[source_block])
            allowed.append(jnp.broadcast_to(listed[offset_step] >= 0, (BLOCK, BLOCK)))
        key_all = jnp.concatenate(key_parts, 0).astype(jnp.float32)
        value_all = jnp.concatenate(value_parts, 0).astype(jnp.float32)
        allowed_all = jnp.concatenate(allowed, 1)
        scores = jnp.einsum('qhd,khd->hqk', queries[block_index].astype(jnp.float32), key_all) * scale
        scores = jnp.where(allowed_all[None], scores, -1e+30)
        highest = lax.optimization_barrier(jnp.max(scores, -1, keepdims=True))
        expo = jnp.exp(scores - highest)
        weights = (expo / lax.optimization_barrier(jnp.sum(expo, -1, keepdims=True))).astype(jnp.bfloat16)
        return jnp.einsum('hqk,khd->qhd', weights.astype(jnp.float32), value_all)
    mixture = lax.map(attend, jnp.arange(NB, dtype=jnp.int32)).reshape(TOKENS, D)
    return mixture.astype(jnp.bfloat16)

def reference(down_queries, down_keys, down_values, up_queries, up_keys, up_values, key_blocks):
    lowered = [attention(down_queries[number], down_keys[number], down_values[number], key_blocks) for number in range(N_SECTION)]
    raised = [attention(up_queries[number], up_keys[number], up_values[number], key_blocks) for number in range(N_SECTION)]
    forward = jnp.stack([raised[0]] + lowered[:-1])
    handed = jnp.stack(raised[1:] + [lowered[-1]])
    return (forward, handed)
```

```python
import functools
import math

import jax
import jax.numpy as jnp
from jax import lax
from jax.experimental import pallas as pl
from jax.experimental.pallas import tpu as pltpu
from jax.sharding import PartitionSpec as P

HEAD_DIM = 64
BLOCK = 128
TILE = 2 * HEAD_DIM
FIELD = 21
ABSENT = -1e30
FACTOR = math.log2(math.e) / math.sqrt(HEAD_DIM)


def lanes():
    return lax.broadcasted_iota(jnp.int32, (BLOCK, TILE), 1)


def by_head(tile, low):
    zero = jnp.zeros_like(tile)
    return jnp.concatenate([jnp.where(low, tile, zero), jnp.where(low, zero, tile)], 0)


def partial(query, key, value, low, low16, causal):
    scores = lax.dot_general(
        query, by_head(key, low16), (((1,), (1,)), ((), ())), preferred_element_type=jnp.float32
    ) * FACTOR
    first, second = scores[:, :BLOCK], scores[:, BLOCK:]
    if causal is not None:
        first = jnp.where(causal, first, ABSENT)
        second = jnp.where(causal, second, ABSENT)
    top_first = jnp.max(first, -1, keepdims=True)
    top_second = jnp.max(second, -1, keepdims=True)
    weights = jnp.concatenate(
        [jnp.exp2(first - top_first), jnp.exp2(second - top_second)], 1
    ).astype(jnp.bfloat16)
    ones = jnp.ones_like(value)
    columns = jnp.concatenate([by_head(value, low16), by_head(ones, low16)], 1)
    sums = jnp.dot(weights, columns, preferred_element_type=jnp.float32)
    return sums[:, :TILE], sums[:, TILE:], jnp.where(low, top_first, top_second)


def pack(logs):
    high = logs.astype(jnp.bfloat16).astype(jnp.float32)
    rest = logs - high
    middle = rest.astype(jnp.bfloat16).astype(jnp.float32)
    last = (rest - middle).astype(jnp.bfloat16).astype(jnp.float32)
    return (high + pltpu.roll(middle, FIELD, 1) + pltpu.roll(last, 2 * FIELD, 1)).astype(jnp.bfloat16)


def unpack(packed, j):
    row = lax.broadcasted_iota(jnp.int32, (TILE, TILE), 0)
    lane = lax.broadcasted_iota(jnp.int32, (TILE, TILE), 1)
    place = row % HEAD_DIM
    piece = (place == j) | (place == j + FIELD) | (place == j + 2 * FIELD)
    pick = jnp.where(piece & (row // HEAD_DIM == lane // HEAD_DIM), 1.0, 0.0).astype(jnp.bfloat16)
    return jnp.dot(packed, pick, preferred_element_type=jnp.float32)


def kernel(tiles, part, flags_ref, query_ref, key_ref, value_ref, *refs):
    if part == 0:
        carried_ref, (out_ref,) = None, refs
    elif part == 1:
        carried_ref, out_ref = refs
    else:
        carried_ref, _, out_ref = refs
    lane = lanes()
    low = lane < HEAD_DIM
    low16 = lax.broadcasted_iota(jnp.int16, (BLOCK, TILE), 1) < HEAD_DIM
    place = lane % HEAD_DIM
    causal = None
    if part == 2:
        causal = lax.broadcasted_iota(jnp.int32, (BLOCK, BLOCK), 0) >= lax.broadcasted_iota(
            jnp.int32, (BLOCK, BLOCK), 1
        )
    if carried_ref is not None:
        packed = carried_ref[:, tiles * TILE :]
        near, far = flags_ref[0, 0] >= 0, flags_ref[0, 1] >= 0
        have = far if part == 1 else near | far

    def step(j, logs):
        columns = pl.ds(pl.multiple_of(j * TILE, TILE), TILE)
        sums, total, top = partial(
            query_ref[:, columns], key_ref[:, columns], value_ref[:, columns], low, low16, causal
        )
        if carried_ref is None:
            out_ref[:, columns] = (sums / total).astype(jnp.bfloat16)
            here = top + jnp.log2(total)
        else:
            came = jnp.where(have, unpack(packed, j), ABSENT)
            if part == 1:
                top = jnp.where(near, top, ABSENT)
            most = jnp.maximum(top, came)
            own, other = jnp.exp2(top - most), jnp.exp2(came - most)
            whole = own * total + other
            out_ref[:, columns] = (
                (own * sums + other * carried_ref[:, columns].astype(jnp.float32)) / whole
            ).astype(jnp.bfloat16)
            here = most + jnp.log2(whole)
        return jnp.where(place == j, here, logs) if part < 2 else logs

    logs = lax.fori_loop(0, tiles, step, jnp.zeros((BLOCK, TILE), jnp.float32))
    if part < 2:
        out_ref[:, tiles * TILE :] = pack(logs)


def attend(part, tiles, first, flags, query, query_first, key, value, carried=None, into=None):
    width = tiles * TILE
    place = lambda start: pl.BlockSpec((BLOCK, width), lambda _: (0, start // tiles))
    operands = [flags, query, key, value]
    specs = [pl.BlockSpec(memory_space=pltpu.SMEM), place(query_first), place(first), place(first)]
    if carried is not None:
        operands.append(carried)
        specs.append(pl.BlockSpec((BLOCK, width + TILE), lambda _: (0, 0)))
    aliases = {}
    if part < 2:
        shape, out_spec = (BLOCK, width + TILE), pl.BlockSpec((BLOCK, width + TILE), lambda _: (0, 0))
    else:
        shape, out_spec = key.shape, place(first)
        operands.append(into)
        specs.append(pl.BlockSpec(memory_space=pl.ANY))
        aliases = {len(operands) - 1: 0}
    flops = tiles * 2 * (2 * BLOCK * BLOCK * TILE * 2)
    return pl.pallas_call(
        functools.partial(kernel, tiles, part),
        grid=(1,),
        out_shape=jax.ShapeDtypeStruct(shape, jnp.bfloat16),
        in_specs=specs,
        out_specs=out_spec,
        input_output_aliases=aliases,
        name=("far", "near", "own")[part],
        compiler_params=pltpu.CompilerParams(vmem_limit_bytes=32 * 1024 * 1024),
        cost_estimate=pl.CostEstimate(
            flops=flops, bytes_accessed=5 * BLOCK * width * 2, transcendentals=tiles * 2 * BLOCK * BLOCK
        ),
    )(*operands)


def shifted(block, axis, distance):
    devices = range(lax.axis_size(axis))
    route = [(i - distance, i) for i in devices if i - distance in devices]
    return lax.ppermute(block, axis, route)


def on_device(down_queries, down_keys, down_values, up_queries, up_keys, up_values, key_blocks):
    spacing = lax.axis_size("ctx") // 4
    groups = (
        tuple(a[0] for a in (down_queries, down_keys, down_values)),
        tuple(a[0] for a in (up_queries, up_keys, up_values)),
    )
    all_tiles = down_queries.shape[2] // TILE
    tiles = all_tiles // 2
    chunks = [(g, first) for first in range(0, all_tiles, tiles) for g in range(2)]
    nearer = lambda x: shifted(x, "ctx", -spacing)
    back = lambda x: shifted(x, "ctx", spacing)
    later_flags = nearer(key_blocks)
    once = [nearer(groups[g][0][:, first * TILE : (first + tiles) * TILE]) for g, first in chunks]
    twice = [nearer(x) for x in once]
    outs = [jnp.zeros_like(groups[0][0]), jnp.zeros_like(groups[0][0])]
    for c, (g, first) in enumerate(chunks):
        _, key, value = groups[g]
        far = attend(0, tiles, first, later_flags, twice[c], 0, key, value)
        near = attend(1, tiles, first, later_flags, once[c], 0, key, value, back(far))
        outs[g] = attend(2, tiles, first, key_blocks, groups[g][0], first, key, value, back(near), outs[g])
    lowered, raised = outs[0][None], outs[1][None]
    section_index = lax.axis_index("section")
    last_section = lax.axis_size("section") - 1
    forward = shifted(lowered, "section", 1)
    forward = jnp.where(section_index == 0, raised, forward)
    handed = shifted(raised, "section", -1)
    handed = jnp.where(section_index == last_section, lowered, handed)
    return (forward, handed)


def solution(mesh):
    placed = (P("section", "ctx", None),) * 6 + (P("ctx", None),)
    return jax.shard_map(
        on_device,
        mesh=mesh,
        in_specs=placed,
        out_specs=(P("section", "ctx", None), P("section", "ctx", None)),
        check_vma=False,
    )
```

```python
import functools
import math

import jax
import jax.numpy as jnp
from jax import lax
from jax.experimental import pallas as pl
from jax.experimental.pallas import tpu as pltpu
from jax.sharding import PartitionSpec as P

HEAD_DIM = 64
BLOCK = 128
TILE = 2 * HEAD_DIM
FIELD = 21
ABSENT = -1e30
WEIGHT = 30
FACTOR = math.log2(math.e) / math.sqrt(HEAD_DIM)
FAR, NEAR, BOTH, OWN = range(4)


def iota(shape, dimension):
    return lax.broadcasted_iota(jnp.int32, shape, dimension)


def by_head(tile, low):
    zero = jnp.zeros_like(tile)
    return jnp.concatenate([jnp.where(low, tile, zero), jnp.where(low, zero, tile)], 0)


def pieces(x, count):
    found = []
    for _ in range(count):
        found.append(x.astype(jnp.bfloat16).astype(jnp.float32))
        x = x - found[-1]
    return found


def fields(parts, tiles):
    within = iota((BLOCK, TILE), 1) % HEAD_DIM < tiles
    packed = jnp.where(within, parts[0], 0.0)
    for place, part in enumerate(parts[1:], 1):
        packed = packed + pltpu.roll(jnp.where(within, part, 0.0), place * FIELD, 1)
    return packed.astype(jnp.bfloat16)


def field_sum(packed, start, count):
    packed = packed.astype(jnp.float32)
    return sum(
        packed if i == 0 else pltpu.roll(packed, TILE - i * FIELD, 1) for i in range(start, start + count)
    )


def spreader():
    row, column = iota((TILE, 2 * TILE), 0), iota((TILE, 2 * TILE), 1)
    place = row % HEAD_DIM
    same = (row // HEAD_DIM == (column // HEAD_DIM) % 2) & (place < 2 * FIELD)
    return jnp.where(same & (column < TILE), place % FIELD, -1).astype(jnp.int16)


def share(query, key, value, low, heads, causal=None):
    scores = lax.dot_general(
        query, by_head(key, low), (((1,), (1,)), ((), ())), preferred_element_type=jnp.float32
    ) * FACTOR
    weights, tops = [], []
    for half in (scores[:, :BLOCK], scores[:, BLOCK:]):
        if causal is not None:
            half = jnp.where(causal, half, ABSENT)
        tops.append(jnp.max(half, -1, keepdims=True))
        weights.append(jnp.exp2(half - tops[-1]).astype(jnp.bfloat16))
    sums = jnp.dot(
        jnp.concatenate(weights, 1),
        jnp.concatenate([by_head(value, low), heads], 1),
        preferred_element_type=jnp.float32,
    )
    return sums[:, :TILE], sums[:, TILE:], tops


def kernel(tiles, first, part, *refs):
    query_ref, key_ref, value_ref, *refs = refs
    width = tiles * TILE
    if part in (NEAR, OWN):
        other_ref, flags_ref, *refs = refs
    elif part == BOTH:
        far_pair_ref, flags_ref, *refs = refs
    if part != FAR:
        sums_ref = refs.pop()
    if part == BOTH:
        far_ref = refs.pop()
    out_ref = refs[-1]
    lane = iota((BLOCK, TILE), 1)
    low = lane < HEAD_DIM
    place = lane % HEAD_DIM
    low16 = lax.broadcasted_iota(jnp.int16, (BLOCK, TILE), 1) < HEAD_DIM
    heads = by_head(jnp.ones((BLOCK, TILE), jnp.bfloat16), low16)
    causal = iota((BLOCK, BLOCK), 0) >= iota((BLOCK, BLOCK), 1) if part == OWN else None
    top = total = far_top = far_total = jnp.zeros((BLOCK, TILE), jnp.float32)
    for j in range(tiles):
        columns = slice(j * TILE, (j + 1) * TILE)
        there = slice((first + j) * TILE, (first + j + 1) * TILE)
        query = query_ref[:, there if part == OWN else columns]
        sums, totals, tops = share(query, key_ref[:, there], value_ref[:, there], low16, heads, causal)
        top = jnp.where(place == j, jnp.where(low, tops[0], tops[1]), top)
        total = jnp.where(place == j, totals, total)
        if part == FAR:
            out_ref[:, columns] = (sums / totals).astype(jnp.bfloat16)
        else:
            sums_ref[:, columns] = sums
        if part == BOTH:
            sums, totals, tops = share(query, far_pair_ref[:BLOCK, columns], far_pair_ref[BLOCK:, columns], low16, heads)
            far_top = jnp.where(place == j, jnp.where(low, tops[0], tops[1]), far_top)
            far_total = jnp.where(place == j, totals, far_total)
            far_ref[:, columns] = sums
    if part != FAR:
        near, far = flags_ref[0:1, :] > 0, flags_ref[1:2, :] > 0
        if part != BOTH:
            far_ref = other_ref
            far_top, far_total = field_sum(other_ref[:, width:], 0, 3), 1.0
        far_top = jnp.where(near | far if part == OWN else far, far_top, ABSENT)
        if part != OWN:
            top = jnp.where(near, top, ABSENT)
        most = jnp.maximum(top, far_top)
        here, there = jnp.exp2(top - most), jnp.exp2(far_top - most)
        top, total = most, here * total + there * far_total
        spread = spreader()
        here, there = fields(pieces(here / total, 2), tiles), fields(pieces(there / total, 2), tiles)
        for j in range(tiles):
            columns = slice(j * TILE, (j + 1) * TILE)
            pick = jnp.where(spread[:, :TILE] == j, 1.0, 0.0).astype(jnp.bfloat16)
            both = jnp.dot(jnp.concatenate([here, there], 0), pick, preferred_element_type=jnp.float32)
            result = both[:BLOCK] * sums_ref[:, columns]
            result = result + both[BLOCK:] * far_ref[:, columns].astype(jnp.float32)
            if part == OWN:
                columns = slice((first + j) * TILE, (first + j + 1) * TILE)
            out_ref[:, columns] = result.astype(jnp.bfloat16)
    if part != OWN:
        out_ref[:, width:] = fields(pieces(top + jnp.log2(total), 3), tiles)


def attend(part, tiles, first, query, key, value, *others):
    width = tiles * TILE
    operands = (query, key, value) + others
    out_shape = key.shape if part == OWN else (BLOCK, width + TILE)
    in_vmem = pl.BlockSpec(memory_space=pltpu.VMEM)
    return pl.pallas_call(
        functools.partial(kernel, tiles, first, part),
        out_shape=jax.ShapeDtypeStruct(out_shape, jnp.bfloat16),
        in_specs=[in_vmem] * len(operands),
        out_specs=in_vmem,
        scratch_shapes=[pltpu.VMEM((BLOCK, width), jnp.float32)] * (0, 1, 2, 1)[part],
        input_output_aliases={len(operands) - 1: 0} if part == OWN and first else {},
        name=("far", "near", "both", "own")[part],
        compiler_params=pltpu.CompilerParams(vmem_limit_bytes=16 * 1024 * 1024),
        cost_estimate=pl.CostEstimate(
            flops=tiles * 8 * BLOCK * BLOCK * TILE * WEIGHT,
            bytes_accessed=5 * BLOCK * width * 2,
            transcendentals=tiles * 2 * BLOCK * BLOCK,
        ),
    )(*operands)


def shifted(block, axis, distance):
    devices = range(lax.axis_size(axis))
    route = [(i - distance, i) for i in devices if i - distance in devices]
    return lax.ppermute(block, axis, route)


def stays(below, above):
    section, size = lax.axis_index("section"), lax.axis_size("section")
    here = jnp.where(section == size - 1, below, above)
    if size > 2:
        here = jnp.where((section == size - 1) | (section == 0), here, shifted(below, "section", 1))
    return here


def crosses(below, above):
    section, size = lax.axis_index("section"), lax.axis_size("section")
    if size == 2:
        return lax.ppermute(jnp.where(section == size - 1, above, below), "section", [(0, 1), (1, 0)])
    return jnp.where(section == size - 1, shifted(below, "section", 1), shifted(above, "section", -1))


def after(x, *others):
    return lax.optimization_barrier((x, *others))[0]


def on_device(down_queries, down_keys, down_values, up_queries, up_keys, up_values, key_blocks):
    spacing = lax.axis_size("ctx") // 4
    onward = lambda x: shifted(x, "ctx", -spacing)
    back = lambda x: shifted(x, "ctx", spacing)
    pairs = tuple((d[0], u[0]) for d, u in ((down_queries, up_queries), (down_keys, up_keys), (down_values, up_values)))
    count = down_queries.shape[2] // TILE
    half = count // 2
    spread_flags = lambda x: jnp.broadcast_to(jnp.where(x >= 0, 1.0, 0.0).astype(jnp.float32).reshape(2, 1), (2, TILE))

    key, value = stays(*pairs[1]), stays(*pairs[2])
    far = back(jnp.concatenate([key, value], 0))
    query2 = crosses(*pairs[0])
    query = stays(*pairs[0])
    key2, value2 = crosses(*pairs[1]), crosses(*pairs[2])
    once_a = onward(query2[:, : half * TILE])
    once_b = onward(query2[:, half * TILE :])
    twice_a = onward(once_a)
    twice_b = onward(after(once_b, once_a))
    once = onward(after(query, once_b))
    flags = spread_flags(key_blocks)
    next_blocks = onward(key_blocks)

    far_a = attend(FAR, half, 0, twice_a, key2, value2)
    back_a = back(far_a)
    far_b = attend(FAR, count - half, half, after(twice_b, far_a, far), key2, value2)
    back_b = back(far_b)
    next_flags = spread_flags(after(next_blocks, far_b))
    near_a = attend(NEAR, half, 0, once_a, key2, value2, after(back_a, far_b), next_flags)
    done_a = back(near_a)
    near_b = attend(NEAR, count - half, half, once_b, key2, value2, after(back_b, near_a), next_flags)
    done_b = back(near_b)
    near = attend(BOTH, count, 0, after(once, near_b), key, value, far, next_flags)
    done = back(near)
    out2 = attend(OWN, half, 0, query2, key2, value2, after(done_a, near), flags)
    out2 = attend(OWN, count - half, half, query2, key2, value2, done_b, flags, out2)
    out = attend(OWN, count, 0, query, key, value, after(done, out2), flags)

    at_end = lax.axis_index("section") == lax.axis_size("section") - 1
    forward = jnp.where(at_end, out2, out)
    handed = jnp.where(at_end, out, out2)
    return forward[None], handed[None]


def solution(mesh):
    placed = (P("section", "ctx", None),) * 6 + (P("ctx", None),)
    return jax.shard_map(
        on_device,
        mesh=mesh,
        in_specs=placed,
        out_specs=(P("section", "ctx", None), P("section", "ctx", None)),
        check_vma=False,
    )
```

```python
import functools
import math

import jax
import jax.numpy as jnp
from jax import lax
from jax.experimental import pallas as pl
from jax.experimental.pallas import tpu as pltpu
from jax.sharding import PartitionSpec as P

HEAD_DIM = 64
BLOCK = 128
TILE = 2 * HEAD_DIM
ABSENT = -1e30
WEIGHT = 30
FACTOR = math.log2(math.e) / math.sqrt(HEAD_DIM)
FAR, NEAR, BOTH, OWN, LOCAL = range(5)


def iota(shape, dimension):
    return lax.broadcasted_iota(jnp.int32, shape, dimension)


def by_head(tile, low):
    zero = jnp.zeros_like(tile)
    return jnp.concatenate([jnp.where(low, tile, zero), jnp.where(low, zero, tile)], 0)


def pieces(x, count):
    found = []
    for _ in range(count):
        found.append(x.astype(jnp.bfloat16).astype(jnp.float32))
        x = x - found[-1]
    return found


def fields(parts, tiles):
    within = iota((BLOCK, TILE), 1) % HEAD_DIM < tiles
    packed = jnp.where(within, parts[0], 0.0)
    for place, part in enumerate(parts[1:], 1):
        packed = packed + pltpu.roll(jnp.where(within, part, 0.0), place * tiles, 1)
    return packed


def spreader(tiles):
    row, column = iota((TILE, TILE), 0), iota((TILE, TILE), 1)
    place = row % HEAD_DIM
    same = (row // HEAD_DIM == column // HEAD_DIM) & (place < 2 * tiles)
    return jnp.where(same, place % tiles, -1).astype(jnp.int16)


def tile_rows(j):
    return slice(j * BLOCK, (j + 1) * BLOCK)


def log_rows(tiles):
    return -(-6 * tiles // 16) * 16 if 6 * tiles <= HEAD_DIM else TILE


def pack(out_ref, logs, tiles):
    packed = fields(pieces(logs, 3), tiles)
    if 6 * tiles <= HEAD_DIM:
        packed = packed + pltpu.roll(packed, TILE - HEAD_DIM + 3 * tiles, 1)
    out_ref[tiles * BLOCK :, :] = packed.T[: log_rows(tiles)].astype(jnp.bfloat16)


def unpack(payload_ref, tiles):
    rows = payload_ref[tiles * BLOCK :, :].astype(jnp.float32)
    if rows.shape[0] < TILE:
        rows = jnp.concatenate([rows, jnp.zeros((TILE - rows.shape[0], BLOCK), jnp.float32)], 0)
    packed = rows.T
    if 6 * tiles <= HEAD_DIM:
        packed = jnp.where(iota((BLOCK, TILE), 1) < HEAD_DIM, packed, pltpu.roll(packed, HEAD_DIM - 3 * tiles, 1))
    return packed + pltpu.roll(packed, TILE - tiles, 1) + pltpu.roll(packed, TILE - 2 * tiles, 1)


def mix(top, total, far_top, far_total, tiles):
    most = jnp.maximum(top, far_top)
    here, there = jnp.exp2(top - most), jnp.exp2(far_top - most)
    whole = here * total + there * far_total
    weights = [fields(pieces(x / whole, 2), tiles).astype(jnp.bfloat16) for x in (here, there)]
    return jnp.concatenate(weights, 0), most + jnp.log2(whole)


def blend(mixed, spread, j, sums_ref, far_ref, columns):
    pick = jnp.where(spread == j, 1.0, 0.0).astype(jnp.bfloat16)
    both = jnp.dot(mixed, pick, preferred_element_type=jnp.float32)
    result = both[:BLOCK] * sums_ref[:, columns] + both[BLOCK:] * far_ref[tile_rows(j), :].astype(jnp.float32)
    return result.astype(jnp.bfloat16)


def share(query, key, value, low, heads, causal=None):
    scores = lax.dot_general(
        query, by_head(key, low), (((1,), (1,)), ((), ())), preferred_element_type=jnp.float32
    ) * FACTOR
    weights, tops = [], []
    for half in (scores[:, :BLOCK], scores[:, BLOCK:]):
        if causal is not None:
            half = jnp.where(causal, half, ABSENT)
        tops.append(jnp.max(half, -1, keepdims=True))
        weights.append(jnp.exp2(half - tops[-1]).astype(jnp.bfloat16))
    sums = jnp.dot(
        jnp.concatenate(weights, 1),
        jnp.concatenate([by_head(value, low), heads], 1),
        preferred_element_type=jnp.float32,
    )
    return sums[:, :TILE], sums[:, TILE:], tops


def kernel(tiles, first, part, *refs):
    query_ref, key_ref, value_ref, *refs = refs
    if part in (NEAR, OWN):
        other_ref, flags_ref, *refs = refs
    elif part == BOTH:
        far_pair_ref, flags_ref, *refs = refs
    if part in (NEAR, BOTH, OWN):
        sums_ref = refs.pop()
    if part == BOTH:
        far_ref = refs.pop()
    out_ref = refs[-1]
    if part == LOCAL:
        sums_ref, state_ref = refs
    lane = iota((BLOCK, TILE), 1)
    low = lane < HEAD_DIM
    place = lane % HEAD_DIM
    low16 = lax.broadcasted_iota(jnp.int16, (BLOCK, TILE), 1) < HEAD_DIM
    heads = by_head(jnp.ones((BLOCK, TILE), jnp.bfloat16), low16)
    causal = iota((BLOCK, BLOCK), 0) >= iota((BLOCK, BLOCK), 1) if part in (OWN, LOCAL) else None
    top = total = far_top = far_total = jnp.zeros((BLOCK, TILE), jnp.float32)
    for j in range(tiles):
        columns = slice(j * TILE, (j + 1) * TILE)
        there = slice((first + j) * TILE, (first + j + 1) * TILE)
        query = query_ref[:, there if part in (OWN, LOCAL) else columns]
        sums, totals, tops = share(query, key_ref[:, there], value_ref[:, there], low16, heads, causal)
        top = jnp.where(place == j, jnp.where(low, tops[0], tops[1]), top)
        total = jnp.where(place == j, totals, total)
        if part == FAR:
            out_ref[tile_rows(j), :] = (sums / totals).astype(jnp.bfloat16)
        else:
            sums_ref[:, columns] = sums
        if part == BOTH:
            sums, totals, tops = share(query, far_pair_ref[:BLOCK, columns], far_pair_ref[BLOCK:, columns], low16, heads)
            far_top = jnp.where(place == j, jnp.where(low, tops[0], tops[1]), far_top)
            far_total = jnp.where(place == j, totals, far_total)
            far_ref[tile_rows(j), :] = sums
    if part == LOCAL:
        state_ref[:, :TILE] = top
        state_ref[:, TILE:] = total
        return
    if part == FAR:
        pack(out_ref, top + jnp.log2(total), tiles)
        return
    near, far = flags_ref[0:1, :] > 0, flags_ref[1:2, :] > 0
    if part != BOTH:
        far_ref = other_ref
        far_top, far_total = unpack(other_ref, tiles), 1.0
    far_top = jnp.where(near | far if part == OWN else far, far_top, ABSENT)
    if part != OWN:
        top = jnp.where(near, top, ABSENT)
    mixed, log = mix(top, total, far_top, far_total, tiles)
    spread = spreader(tiles)
    for j in range(tiles):
        columns = slice(j * TILE, (j + 1) * TILE)
        result = blend(mixed, spread, j, sums_ref, far_ref, columns)
        if part == OWN:
            out_ref[:, (first + j) * TILE : (first + j + 1) * TILE] = result
        else:
            out_ref[tile_rows(j), :] = result
    if part != OWN:
        pack(out_ref, log, tiles)


def attend(part, tiles, first, query, key, value, *others):
    width = tiles * TILE
    operands = (query, key, value) + others
    if part == OWN:
        out_shape = jax.ShapeDtypeStruct(key.shape, jnp.bfloat16)
    elif part == LOCAL:
        out_shape = tuple(jax.ShapeDtypeStruct((BLOCK, w), jnp.float32) for w in (width, 2 * TILE))
    else:
        out_shape = jax.ShapeDtypeStruct((tiles * BLOCK + log_rows(tiles), TILE), jnp.bfloat16)
    in_vmem = pl.BlockSpec(memory_space=pltpu.VMEM)
    return pl.pallas_call(
        functools.partial(kernel, tiles, first, part),
        out_shape=out_shape,
        in_specs=[in_vmem] * len(operands),
        out_specs=(in_vmem, in_vmem) if part == LOCAL else in_vmem,
        scratch_shapes={
            FAR: (),
            NEAR: (pltpu.VMEM((BLOCK, width), jnp.float32),),
            BOTH: (pltpu.VMEM((tiles * BLOCK, TILE), jnp.float32), pltpu.VMEM((BLOCK, width), jnp.float32)),
            OWN: (pltpu.VMEM((BLOCK, width), jnp.float32),),
            LOCAL: (),
        }[part],
        input_output_aliases={len(operands) - 1: 0} if part == OWN and first else {},
        name=("far", "near", "both", "own", "local")[part],
        compiler_params=pltpu.CompilerParams(vmem_limit_bytes=16 * 1024 * 1024),
        cost_estimate=pl.CostEstimate(
            flops=tiles * 8 * BLOCK * BLOCK * TILE * WEIGHT,
            bytes_accessed=5 * BLOCK * width * 2,
            transcendentals=tiles * 2 * BLOCK * BLOCK,
        ),
    )(*operands)


def last_kernel(count, sums_ref, state_ref, other_ref, flags_ref, second_ref, forward_ref, handed_ref, first_ref, sems):
    at_end = lax.axis_index("section") == lax.axis_size("section") - 1
    step = -(-count // 3) * TILE

    def copy(i, first_out, second_out):
        if i == 0:
            return pltpu.make_async_copy(second_ref, second_out.at[0], sems.at[0])
        cut = slice((i - 1) * step, min(i * step, count * TILE))
        return pltpu.make_async_copy(first_ref.at[:, cut], first_out.at[0, :, cut], sems.at[i])

    def at_place(act):
        pl.when(at_end)(lambda: act(handed_ref, forward_ref))
        pl.when(jnp.logical_not(at_end))(lambda: act(forward_ref, handed_ref))

    at_place(lambda *outs: copy(0, *outs).start())
    there = unpack(other_ref, count)
    there = jnp.where((flags_ref[0:1, :] > 0) | (flags_ref[1:2, :] > 0), there, ABSENT)
    mixed, _ = mix(state_ref[:, :TILE], state_ref[:, TILE:], there, 1.0, count)
    spread = spreader(count)
    for j in range(count):
        columns = slice(j * TILE, (j + 1) * TILE)
        first_ref[:, columns] = blend(mixed, spread, j, sums_ref, other_ref, columns)
        if (j + 1) * TILE % step == 0 or j == count - 1:
            at_place(lambda *outs, i=j * TILE // step + 1: copy(i, *outs).start())

    def wait(*outs):
        for i in range(-(-count * TILE // step) + 1):
            copy(i, *outs).wait()

    at_place(wait)


def finish(sums, state, came, flags, second):
    in_vmem, anywhere = pl.BlockSpec(memory_space=pltpu.VMEM), pl.BlockSpec(memory_space=pl.ANY)
    out = jax.ShapeDtypeStruct((1,) + second.shape, second.dtype)
    return pl.pallas_call(
        functools.partial(last_kernel, second.shape[1] // TILE),
        out_shape=(out, out),
        in_specs=[in_vmem] * 5,
        out_specs=(anywhere, anywhere),
        scratch_shapes=[pltpu.VMEM(second.shape, second.dtype), pltpu.SemaphoreType.DMA((4,))],
        name="last",
        compiler_params=pltpu.CompilerParams(vmem_limit_bytes=16 * 1024 * 1024),
        cost_estimate=pl.CostEstimate(flops=WEIGHT << 26, bytes_accessed=5 * second.size, transcendentals=0),
    )(sums, state, came, flags, second)


def shifted(block, axis, distance):
    devices = range(lax.axis_size(axis))
    route = [(i - distance, i) for i in devices if i - distance in devices]
    return lax.ppermute(block, axis, route)


def stays(below, above):
    section, size = lax.axis_index("section"), lax.axis_size("section")
    here = jnp.where(section == size - 1, below, above)
    if size > 2:
        here = jnp.where((section == size - 1) | (section == 0), here, shifted(below, "section", 1))
    return here


def crosses(below, above):
    section, size = lax.axis_index("section"), lax.axis_size("section")
    if size == 2:
        return lax.ppermute(jnp.where(section == size - 1, above, below), "section", [(0, 1), (1, 0)])
    return jnp.where(section == size - 1, shifted(below, "section", 1), shifted(above, "section", -1))


def after(x, *others):
    return lax.optimization_barrier((x, *others))[0]


def on_device(down_queries, down_keys, down_values, up_queries, up_keys, up_values, key_blocks):
    spacing = lax.axis_size("ctx") // 4
    onward = lambda x: shifted(x, "ctx", -spacing)
    back = lambda x: shifted(x, "ctx", spacing)
    pairs = tuple((d[0], u[0]) for d, u in ((down_queries, up_queries), (down_keys, up_keys), (down_values, up_values)))
    count = down_queries.shape[2] // TILE
    half = count // 2
    spread_flags = lambda x: jnp.broadcast_to(jnp.where(x >= 0, 1.0, 0.0).astype(jnp.float32).reshape(2, 1), (2, TILE))

    key, value = stays(*pairs[1]), stays(*pairs[2])
    far = back(jnp.concatenate([key, value], 0))
    query2 = crosses(*pairs[0])
    query = stays(*pairs[0])
    key2, value2 = crosses(*pairs[1]), crosses(*pairs[2])
    once_a = onward(query2[:, : half * TILE])
    once_b = onward(query2[:, half * TILE :])
    twice_a = onward(once_a)
    twice_b = onward(after(once_b, once_a))
    flags = spread_flags(key_blocks)
    next_blocks = onward(key_blocks)

    far_a = attend(FAR, half, 0, twice_a, key2, value2)
    back_a = back(far_a)
    once = onward(after(query, far_a))
    far_b = attend(FAR, count - half, half, after(twice_b, far_a, far), key2, value2)
    back_b = back(far_b)
    next_flags = spread_flags(after(next_blocks, far_b))
    near_a = attend(NEAR, half, 0, once_a, key2, value2, after(back_a, far_b), next_flags)
    done_a = back(near_a)
    near_b = attend(NEAR, count - half, half, once_b, key2, value2, after(back_b, near_a), next_flags)
    done_b = back(near_b)
    near = attend(BOTH, count, 0, after(once, near_b), key, value, far, next_flags)
    done = back(near)
    out2 = attend(OWN, half, 0, query2, key2, value2, after(done_a, near), flags)
    out2 = attend(OWN, count - half, half, query2, key2, value2, done_b, flags, out2)
    sums, state = attend(LOCAL, count, 0, after(query, out2), key, value)
    return finish(sums, state, after(done, sums), flags, out2)


def solution(mesh):
    placed = (P("section", "ctx", None),) * 6 + (P("ctx", None),)
    return jax.shard_map(
        on_device,
        mesh=mesh,
        in_specs=placed,
        out_specs=(P("section", "ctx", None), P("section", "ctx", None)),
        check_vma=False,
    )
```

```python
import functools
import math

import jax
import jax.numpy as jnp
from jax import lax
from jax.experimental import pallas as pl
from jax.experimental.pallas import tpu as pltpu
from jax.sharding import PartitionSpec as P

HEAD_DIM = 64
BLOCK = 128
TILE = 2 * HEAD_DIM
ABSENT = -1e30
WEIGHT = 30
FACTOR = math.log2(math.e) / math.sqrt(HEAD_DIM)
FAR, NEAR, BOTH, OWN, LOCAL = range(5)


def iota(shape, dimension):
    return lax.broadcasted_iota(jnp.int32, shape, dimension)


def by_head(tile, low):
    zero = jnp.zeros_like(tile)
    return jnp.concatenate([jnp.where(low, tile, zero), jnp.where(low, zero, tile)], 0)


def pieces(x, count):
    found = []
    for _ in range(count):
        found.append(x.astype(jnp.bfloat16).astype(jnp.float32))
        x = x - found[-1]
    return found


def fields(parts, tiles):
    within = iota((BLOCK, TILE), 1) % HEAD_DIM < tiles
    packed = jnp.where(within, parts[0], 0.0)
    for place, part in enumerate(parts[1:], 1):
        packed = packed + pltpu.roll(jnp.where(within, part, 0.0), place * tiles, 1)
    return packed


def spreader(tiles):
    row, column = iota((TILE, TILE), 0), iota((TILE, TILE), 1)
    place = row % HEAD_DIM
    same = (row // HEAD_DIM == column // HEAD_DIM) & (place < 2 * tiles)
    return jnp.where(same, place % tiles, -1).astype(jnp.int16)


def tile_rows(j):
    return slice(j * BLOCK, (j + 1) * BLOCK)


def log_rows(tiles):
    return -(-6 * tiles // 16) * 16 if 6 * tiles <= HEAD_DIM else TILE


def pack(out_ref, logs, tiles):
    packed = fields(pieces(logs, 3), tiles)
    if 6 * tiles <= HEAD_DIM:
        packed = packed + pltpu.roll(packed, TILE - HEAD_DIM + 3 * tiles, 1)
    out_ref[tiles * BLOCK :, :] = packed.T[: log_rows(tiles)].astype(jnp.bfloat16)


def unpack(payload_ref, tiles):
    rows = payload_ref[tiles * BLOCK :, :].astype(jnp.float32)
    if rows.shape[0] < TILE:
        rows = jnp.concatenate([rows, jnp.zeros((TILE - rows.shape[0], BLOCK), jnp.float32)], 0)
    packed = rows.T
    if 6 * tiles <= HEAD_DIM:
        packed = jnp.where(iota((BLOCK, TILE), 1) < HEAD_DIM, packed, pltpu.roll(packed, HEAD_DIM - 3 * tiles, 1))
    return packed + pltpu.roll(packed, TILE - tiles, 1) + pltpu.roll(packed, TILE - 2 * tiles, 1)


def mix(top, total, far_top, far_total, tiles):
    most = jnp.maximum(top, far_top)
    here, there = jnp.exp2(top - most), jnp.exp2(far_top - most)
    whole = here * total + there * far_total
    weights = [fields(pieces(x / whole, 2), tiles).astype(jnp.bfloat16) for x in (here, there)]
    return jnp.concatenate(weights, 0), most + jnp.log2(whole)


def blend(mixed, spread, j, sums_ref, far_ref, columns):
    pick = jnp.where(spread == j, 1.0, 0.0).astype(jnp.bfloat16)
    both = jnp.dot(mixed, pick, preferred_element_type=jnp.float32)
    result = both[:BLOCK] * sums_ref[:, columns] + both[BLOCK:] * far_ref[tile_rows(j), :].astype(jnp.float32)
    return result.astype(jnp.bfloat16)


def share(query, key, value, low, heads, causal=None):
    scores = lax.dot_general(
        query, by_head(key, low), (((1,), (1,)), ((), ())), preferred_element_type=jnp.float32
    ) * FACTOR
    weights, tops = [], []
    for half in (scores[:, :BLOCK], scores[:, BLOCK:]):
        if causal is not None:
            half = jnp.where(causal, half, ABSENT)
        tops.append(jnp.max(half, -1, keepdims=True))
        weights.append(jnp.exp2(half - tops[-1]).astype(jnp.bfloat16))
    sums = jnp.dot(
        jnp.concatenate(weights, 1),
        jnp.concatenate([by_head(value, low), heads], 1),
        preferred_element_type=jnp.float32,
    )
    return sums[:, :TILE], sums[:, TILE:], tops


def kernel(tiles, first, part, *refs):
    query_ref, key_ref, value_ref, *refs = refs
    if part in (NEAR, OWN):
        other_ref, flags_ref, *refs = refs
    elif part == BOTH:
        far_pair_ref, flags_ref, *refs = refs
    if part in (NEAR, BOTH, OWN):
        sums_ref = refs.pop()
    if part == BOTH:
        far_ref = refs.pop()
    out_ref = refs[-1]
    if part == LOCAL:
        sums_ref, state_ref = refs
    lane = iota((BLOCK, TILE), 1)
    low = lane < HEAD_DIM
    place = lane % HEAD_DIM
    low16 = lax.broadcasted_iota(jnp.int16, (BLOCK, TILE), 1) < HEAD_DIM
    heads = by_head(jnp.ones((BLOCK, TILE), jnp.bfloat16), low16)
    causal = iota((BLOCK, BLOCK), 0) >= iota((BLOCK, BLOCK), 1) if part in (OWN, LOCAL) else None
    top = total = far_top = far_total = jnp.zeros((BLOCK, TILE), jnp.float32)
    for j in range(tiles):
        columns = slice(j * TILE, (j + 1) * TILE)
        there = slice((first + j) * TILE, (first + j + 1) * TILE)
        query = query_ref[:, there if part in (OWN, LOCAL) else columns]
        sums, totals, tops = share(query, key_ref[:, there], value_ref[:, there], low16, heads, causal)
        top = jnp.where(place == j, jnp.where(low, tops[0], tops[1]), top)
        total = jnp.where(place == j, totals, total)
        if part == FAR:
            out_ref[tile_rows(j), :] = (sums / totals).astype(jnp.bfloat16)
        else:
            sums_ref[:, columns] = sums
        if part == BOTH:
            sums, totals, tops = share(query, far_pair_ref[:BLOCK, there], far_pair_ref[BLOCK:, there], low16, heads)
            far_top = jnp.where(place == j, jnp.where(low, tops[0], tops[1]), far_top)
            far_total = jnp.where(place == j, totals, far_total)
            far_ref[tile_rows(j), :] = sums
    if part == LOCAL:
        state_ref[:, :TILE] = top
        state_ref[:, TILE:] = total
        return
    if part == FAR:
        pack(out_ref, top + jnp.log2(total), tiles)
        return
    near, far = flags_ref[0:1, :] > 0, flags_ref[1:2, :] > 0
    if part != BOTH:
        far_ref = other_ref
        far_top, far_total = unpack(other_ref, tiles), 1.0
    far_top = jnp.where(near | far if part == OWN else far, far_top, ABSENT)
    if part != OWN:
        top = jnp.where(near, top, ABSENT)
    mixed, log = mix(top, total, far_top, far_total, tiles)
    spread = spreader(tiles)
    for j in range(tiles):
        columns = slice(j * TILE, (j + 1) * TILE)
        result = blend(mixed, spread, j, sums_ref, far_ref, columns)
        if part == OWN:
            out_ref[:, (first + j) * TILE : (first + j + 1) * TILE] = result
        else:
            out_ref[tile_rows(j), :] = result
    if part != OWN:
        pack(out_ref, log, tiles)


def attend(part, tiles, first, query, key, value, *others):
    width = tiles * TILE
    operands = (query, key, value) + others
    if part == OWN:
        out_shape = jax.ShapeDtypeStruct(key.shape, jnp.bfloat16)
    elif part == LOCAL:
        out_shape = tuple(jax.ShapeDtypeStruct((BLOCK, w), jnp.float32) for w in (width, 2 * TILE))
    else:
        out_shape = jax.ShapeDtypeStruct((tiles * BLOCK + log_rows(tiles), TILE), jnp.bfloat16)
    in_vmem = pl.BlockSpec(memory_space=pltpu.VMEM)
    return pl.pallas_call(
        functools.partial(kernel, tiles, first, part),
        out_shape=out_shape,
        in_specs=[in_vmem] * len(operands),
        out_specs=(in_vmem, in_vmem) if part == LOCAL else in_vmem,
        scratch_shapes={
            FAR: (),
            NEAR: (pltpu.VMEM((BLOCK, width), jnp.float32),),
            BOTH: (pltpu.VMEM((tiles * BLOCK, TILE), jnp.float32), pltpu.VMEM((BLOCK, width), jnp.float32)),
            OWN: (pltpu.VMEM((BLOCK, width), jnp.float32),),
            LOCAL: (),
        }[part],
        input_output_aliases={len(operands) - 1: 0} if part == OWN and first else {},
        name=("far", "near", "both", "own", "local")[part],
        compiler_params=pltpu.CompilerParams(vmem_limit_bytes=16 * 1024 * 1024),
        cost_estimate=pl.CostEstimate(
            flops=tiles * 8 * BLOCK * BLOCK * TILE * WEIGHT,
            bytes_accessed=5 * BLOCK * width * 2,
            transcendentals=tiles * 2 * BLOCK * BLOCK,
        ),
    )(*operands)


def last_kernel(begin, count, sums_ref, state_ref, other_ref, flags_ref, first_ref, second_ref, forward_ref, handed_ref, rest_ref, sems):
    at_end = lax.axis_index("section") == lax.axis_size("section") - 1
    tiles = count - begin
    step = -(-tiles // 3) * TILE
    done = slice(0, begin * TILE)

    def copy(i, first_out, second_out):
        if i == 0:
            return pltpu.make_async_copy(first_ref, first_out.at[0], sems.at[0])
        if i == 1:
            return pltpu.make_async_copy(second_ref.at[:, done], second_out.at[0, :, done], sems.at[1])
        cut = slice((i - 2) * step, min((i - 1) * step, tiles * TILE))
        there = slice(begin * TILE + cut.start, begin * TILE + cut.stop)
        return pltpu.make_async_copy(rest_ref.at[:, cut], second_out.at[0, :, there], sems.at[i])

    def at_place(act):
        pl.when(at_end)(lambda: act(forward_ref, handed_ref))
        pl.when(jnp.logical_not(at_end))(lambda: act(handed_ref, forward_ref))

    def start(numbers):
        def act(*outs):
            for i in numbers:
                copy(i, *outs).start()

        at_place(act)

    def wait(*outs):
        for i in range(-(-tiles * TILE // step) + 2):
            copy(i, *outs).wait()

    start((0, 1))
    there = unpack(other_ref, tiles)
    there = jnp.where((flags_ref[0:1, :] > 0) | (flags_ref[1:2, :] > 0), there, ABSENT)
    mixed, _ = mix(state_ref[:, :TILE], state_ref[:, TILE:], there, 1.0, tiles)
    spread = spreader(tiles)
    for j in range(tiles):
        columns = slice(j * TILE, (j + 1) * TILE)
        rest_ref[:, columns] = blend(mixed, spread, j, sums_ref, other_ref, columns)
        if (j + 1) * TILE % step == 0 or j == tiles - 1:
            start((j * TILE // step + 2,))
    at_place(wait)


def finish(begin, sums, state, came, flags, first, second):
    in_vmem, anywhere = pl.BlockSpec(memory_space=pltpu.VMEM), pl.BlockSpec(memory_space=pl.ANY)
    out = jax.ShapeDtypeStruct((1,) + second.shape, second.dtype)
    count = second.shape[1] // TILE
    return pl.pallas_call(
        functools.partial(last_kernel, begin, count),
        out_shape=(out, out),
        in_specs=[in_vmem] * 6,
        out_specs=(anywhere, anywhere),
        scratch_shapes=[pltpu.VMEM((BLOCK, (count - begin) * TILE), second.dtype), pltpu.SemaphoreType.DMA((5,))],
        name="last",
        compiler_params=pltpu.CompilerParams(vmem_limit_bytes=16 * 1024 * 1024),
        cost_estimate=pl.CostEstimate(flops=WEIGHT << 26, bytes_accessed=5 * second.size, transcendentals=0),
    )(sums, state, came, flags, first, second)


def shifted(block, axis, distance):
    devices = range(lax.axis_size(axis))
    route = [(i - distance, i) for i in devices if i - distance in devices]
    return lax.ppermute(block, axis, route)


def stays(below, above):
    section, size = lax.axis_index("section"), lax.axis_size("section")
    here = jnp.where(section == size - 1, below, above)
    if size > 2:
        here = jnp.where((section == size - 1) | (section == 0), here, shifted(below, "section", 1))
    return here


def crosses(below, above):
    section, size = lax.axis_index("section"), lax.axis_size("section")
    if size == 2:
        return lax.ppermute(jnp.where(section == size - 1, above, below), "section", [(0, 1), (1, 0)])
    return jnp.where(section == size - 1, shifted(below, "section", 1), shifted(above, "section", -1))


def after(x, *others):
    return lax.optimization_barrier((x, *others))[0]


def on_device(down_queries, down_keys, down_values, up_queries, up_keys, up_values, key_blocks):
    spacing = lax.axis_size("ctx") // 4
    onward = lambda x: shifted(x, "ctx", -spacing)
    back = lambda x: shifted(x, "ctx", spacing)
    pairs = tuple((d[0], u[0]) for d, u in ((down_queries, up_queries), (down_keys, up_keys), (down_values, up_values)))
    count = down_queries.shape[2] // TILE
    half = count // 2
    spread_flags = lambda x: jnp.broadcast_to(jnp.where(x >= 0, 1.0, 0.0).astype(jnp.float32).reshape(2, 1), (2, TILE))

    key, value = stays(*pairs[1]), stays(*pairs[2])
    far = back(jnp.concatenate([key, value], 0))
    query2 = crosses(*pairs[0])
    query = stays(*pairs[0])
    key2, value2 = crosses(*pairs[1]), crosses(*pairs[2])
    once_a = onward(query2[:, : half * TILE])
    once_b = onward(query2[:, half * TILE :])
    twice_a = onward(once_a)
    twice_b = onward(after(once_b, once_a))
    flags = spread_flags(key_blocks)
    next_blocks = onward(key_blocks)

    far_a = attend(FAR, half, 0, twice_a, key2, value2)
    back_a = back(far_a)
    once = onward(after(query, far_a))
    far_b = attend(FAR, count - half, half, after(twice_b, far_a, far), key2, value2)
    back_b = back(far_b)
    next_flags = spread_flags(after(next_blocks, far_b))
    near_a = attend(NEAR, half, 0, once_a, key2, value2, after(back_a, far_b), next_flags)
    done_a = back(near_a)
    near_b = attend(NEAR, count - half, half, once_b, key2, value2, after(back_b, near_a), next_flags)
    done_b = back(near_b)
    near_c = attend(BOTH, half, 0, after(once[:, : half * TILE], near_b), key, value, far, next_flags)
    done_c = back(near_c)
    near_d = attend(BOTH, count - half, half, after(once[:, half * TILE :], near_c), key, value, far, next_flags)
    done_d = back(near_d)
    out2 = attend(OWN, half, 0, query2, key2, value2, after(done_a, near_d), flags)
    out2 = attend(OWN, count - half, half, query2, key2, value2, done_b, flags, out2)
    sums, state = attend(LOCAL, count - half, half, after(query, out2), key, value)
    out = attend(OWN, half, 0, query, key, value, after(done_c, sums), flags)
    return finish(half, sums, state, after(done_d, out), flags, out2, out)


def solution(mesh):
    placed = (P("section", "ctx", None),) * 6 + (P("ctx", None),)
    return jax.shard_map(
        on_device,
        mesh=mesh,
        in_specs=placed,
        out_specs=(P("section", "ctx", None), P("section", "ctx", None)),
        check_vma=False,
    )
```

```python
import functools
import math

import jax
import jax.numpy as jnp
from jax import lax
from jax.experimental import pallas as pl
from jax.experimental.pallas import tpu as pltpu
from jax.sharding import PartitionSpec as P

HEAD_DIM = 64
BLOCK = 128
TILE = 2 * HEAD_DIM
ABSENT = -1e30
WEIGHT = 30
FACTOR = math.log2(math.e) / math.sqrt(HEAD_DIM)
FAR, NEAR, BOTH, OWN, LOCAL = range(5)


def iota(shape, dimension):
    return lax.broadcasted_iota(jnp.int32, shape, dimension)


def by_head(tile, low):
    zero = jnp.zeros_like(tile)
    return jnp.concatenate([jnp.where(low, tile, zero), jnp.where(low, zero, tile)], 0)


def pieces(x, count):
    found = []
    for _ in range(count):
        found.append(x.astype(jnp.bfloat16).astype(jnp.float32))
        x = x - found[-1]
    return found


def fields(parts, tiles):
    within = iota((BLOCK, TILE), 1) % HEAD_DIM < tiles
    packed = jnp.where(within, parts[0], 0.0)
    for place, part in enumerate(parts[1:], 1):
        packed = packed + pltpu.roll(jnp.where(within, part, 0.0), place * tiles, 1)
    return packed


def spreader(tiles):
    row, column = iota((TILE, TILE), 0), iota((TILE, TILE), 1)
    place = row % HEAD_DIM
    same = (row // HEAD_DIM == column // HEAD_DIM) & (place < 2 * tiles)
    return jnp.where(same, place % tiles, -1).astype(jnp.int16)


def tile_rows(j):
    return slice(j * BLOCK, (j + 1) * BLOCK)


def log_rows(tiles):
    return -(-6 * tiles // 16) * 16 if 6 * tiles <= HEAD_DIM else TILE


def pack(out_ref, logs, tiles):
    packed = fields(pieces(logs, 3), tiles)
    if 6 * tiles <= HEAD_DIM:
        packed = packed + pltpu.roll(packed, TILE - HEAD_DIM + 3 * tiles, 1)
    out_ref[tiles * BLOCK :, :] = packed.T[: log_rows(tiles)].astype(jnp.bfloat16)


def unpack(payload_ref, tiles):
    rows = payload_ref[tiles * BLOCK :, :].astype(jnp.float32)
    if rows.shape[0] < TILE:
        rows = jnp.concatenate([rows, jnp.zeros((TILE - rows.shape[0], BLOCK), jnp.float32)], 0)
    packed = rows.T
    if 6 * tiles <= HEAD_DIM:
        packed = jnp.where(iota((BLOCK, TILE), 1) < HEAD_DIM, packed, pltpu.roll(packed, HEAD_DIM - 3 * tiles, 1))
    return packed + pltpu.roll(packed, TILE - tiles, 1) + pltpu.roll(packed, TILE - 2 * tiles, 1)


def mix(top, total, far_top, far_total, tiles):
    most = jnp.maximum(top, far_top)
    here, there = jnp.exp2(top - most), jnp.exp2(far_top - most)
    whole = here * total + there * far_total
    weights = [fields(pieces(x / whole, 2), tiles).astype(jnp.bfloat16) for x in (here, there)]
    return jnp.concatenate(weights, 0), most + jnp.log2(whole)


def blend(mixed, spread, j, sums_ref, far_ref, columns):
    pick = jnp.where(spread == j, 1.0, 0.0).astype(jnp.bfloat16)
    both = jnp.dot(mixed, pick, preferred_element_type=jnp.float32)
    result = both[:BLOCK] * sums_ref[:, columns] + both[BLOCK:] * far_ref[tile_rows(j), :].astype(jnp.float32)
    return result.astype(jnp.bfloat16)


def share(query, key, value, low, heads, causal=None):
    scores = lax.dot_general(
        query, by_head(key, low), (((1,), (1,)), ((), ())), preferred_element_type=jnp.float32
    ) * FACTOR
    weights, tops = [], []
    for half in (scores[:, :BLOCK], scores[:, BLOCK:]):
        if causal is not None:
            half = jnp.where(causal, half, ABSENT)
        tops.append(jnp.max(half, -1, keepdims=True))
        weights.append(jnp.exp2(half - tops[-1]).astype(jnp.bfloat16))
    sums = jnp.dot(
        jnp.concatenate(weights, 1),
        jnp.concatenate([by_head(value, low), heads], 1),
        preferred_element_type=jnp.float32,
    )
    return sums[:, :TILE], sums[:, TILE:], tops


def kernel(tiles, first, part, *refs):
    query_ref, key_ref, value_ref, *refs = refs
    if part in (NEAR, OWN):
        other_ref, flags_ref, *refs = refs
    elif part == BOTH:
        far_pair_ref, flags_ref, *refs = refs
    if part in (NEAR, BOTH, OWN):
        sums_ref = refs.pop()
    if part == BOTH:
        far_ref = refs.pop()
    out_ref = refs[-1]
    if part == LOCAL:
        sums_ref, state_ref = refs
    lane = iota((BLOCK, TILE), 1)
    low = lane < HEAD_DIM
    place = lane % HEAD_DIM
    low16 = lax.broadcasted_iota(jnp.int16, (BLOCK, TILE), 1) < HEAD_DIM
    heads = by_head(jnp.ones((BLOCK, TILE), jnp.bfloat16), low16)
    causal = iota((BLOCK, BLOCK), 0) >= iota((BLOCK, BLOCK), 1) if part in (OWN, LOCAL) else None
    top = total = far_top = far_total = jnp.zeros((BLOCK, TILE), jnp.float32)
    for j in range(tiles):
        columns = slice(j * TILE, (j + 1) * TILE)
        there = slice((first + j) * TILE, (first + j + 1) * TILE)
        query = query_ref[:, there if part in (OWN, LOCAL) else columns]
        sums, totals, tops = share(query, key_ref[:, there], value_ref[:, there], low16, heads, causal)
        top = jnp.where(place == j, jnp.where(low, tops[0], tops[1]), top)
        total = jnp.where(place == j, totals, total)
        if part == FAR:
            out_ref[tile_rows(j), :] = (sums / totals).astype(jnp.bfloat16)
        else:
            sums_ref[:, columns] = sums
        if part == BOTH:
            sums, totals, tops = share(query, far_pair_ref[:BLOCK, columns], far_pair_ref[BLOCK:, columns], low16, heads)
            far_top = jnp.where(place == j, jnp.where(low, tops[0], tops[1]), far_top)
            far_total = jnp.where(place == j, totals, far_total)
            far_ref[tile_rows(j), :] = sums
    if part == LOCAL:
        state_ref[:, :TILE] = top
        state_ref[:, TILE:] = total
        return
    if part == FAR:
        pack(out_ref, top + jnp.log2(total), tiles)
        return
    near, far = flags_ref[0:1, :] > 0, flags_ref[1:2, :] > 0
    if part != BOTH:
        far_ref = other_ref
        far_top, far_total = unpack(other_ref, tiles), 1.0
    far_top = jnp.where(near | far if part == OWN else far, far_top, ABSENT)
    if part != OWN:
        top = jnp.where(near, top, ABSENT)
    mixed, log = mix(top, total, far_top, far_total, tiles)
    spread = spreader(tiles)
    for j in range(tiles):
        columns = slice(j * TILE, (j + 1) * TILE)
        result = blend(mixed, spread, j, sums_ref, far_ref, columns)
        if part == OWN:
            out_ref[:, (first + j) * TILE : (first + j + 1) * TILE] = result
        else:
            out_ref[tile_rows(j), :] = result
    if part != OWN:
        pack(out_ref, log, tiles)


def attend(part, tiles, first, query, key, value, *others):
    width = tiles * TILE
    operands = (query, key, value) + others
    if part == OWN:
        out_shape = jax.ShapeDtypeStruct(key.shape, jnp.bfloat16)
    elif part == LOCAL:
        out_shape = tuple(jax.ShapeDtypeStruct((BLOCK, w), jnp.float32) for w in (width, 2 * TILE))
    else:
        out_shape = jax.ShapeDtypeStruct((tiles * BLOCK + log_rows(tiles), TILE), jnp.bfloat16)
    in_vmem = pl.BlockSpec(memory_space=pltpu.VMEM)
    return pl.pallas_call(
        functools.partial(kernel, tiles, first, part),
        out_shape=out_shape,
        in_specs=[in_vmem] * len(operands),
        out_specs=(in_vmem, in_vmem) if part == LOCAL else in_vmem,
        scratch_shapes={
            FAR: (),
            NEAR: (pltpu.VMEM((BLOCK, width), jnp.float32),),
            BOTH: (pltpu.VMEM((tiles * BLOCK, TILE), jnp.float32), pltpu.VMEM((BLOCK, width), jnp.float32)),
            OWN: (pltpu.VMEM((BLOCK, width), jnp.float32),),
            LOCAL: (),
        }[part],
        input_output_aliases={len(operands) - 1: 0} if part == OWN and first else {},
        name=("far", "near", "both", "own", "local")[part],
        compiler_params=pltpu.CompilerParams(vmem_limit_bytes=16 * 1024 * 1024),
        cost_estimate=pl.CostEstimate(
            flops=tiles * 8 * BLOCK * BLOCK * TILE * WEIGHT,
            bytes_accessed=5 * BLOCK * width * 2,
            transcendentals=tiles * 2 * BLOCK * BLOCK,
        ),
    )(*operands)


def last_kernel(count, sums_ref, state_ref, other_ref, flags_ref, second_ref, forward_ref, handed_ref, first_ref, sems):
    at_end = lax.axis_index("section") == lax.axis_size("section") - 1
    step = -(-count // 6) * TILE

    def copy(i, first_out, second_out):
        if i == 0:
            return pltpu.make_async_copy(second_ref, second_out.at[0], sems.at[0])
        cut = slice((i - 1) * step, min(i * step, count * TILE))
        return pltpu.make_async_copy(first_ref.at[:, cut], first_out.at[0, :, cut], sems.at[i])

    def at_place(act):
        pl.when(at_end)(lambda: act(handed_ref, forward_ref))
        pl.when(jnp.logical_not(at_end))(lambda: act(forward_ref, handed_ref))

    at_place(lambda *outs: copy(0, *outs).start())
    there = unpack(other_ref, count)
    there = jnp.where((flags_ref[0:1, :] > 0) | (flags_ref[1:2, :] > 0), there, ABSENT)
    mixed, _ = mix(state_ref[:, :TILE], state_ref[:, TILE:], there, 1.0, count)
    spread = spreader(count)
    for j in range(count):
        columns = slice(j * TILE, (j + 1) * TILE)
        first_ref[:, columns] = blend(mixed, spread, j, sums_ref, other_ref, columns)
        if (j + 1) * TILE % step == 0 or j == count - 1:
            at_place(lambda *outs, i=j * TILE // step + 1: copy(i, *outs).start())

    def wait(*outs):
        for i in range(-(-count * TILE // step) + 1):
            copy(i, *outs).wait()

    at_place(wait)


def finish(sums, state, came, flags, second):
    in_vmem, anywhere = pl.BlockSpec(memory_space=pltpu.VMEM), pl.BlockSpec(memory_space=pl.ANY)
    out = jax.ShapeDtypeStruct((1,) + second.shape, second.dtype)
    return pl.pallas_call(
        functools.partial(last_kernel, second.shape[1] // TILE),
        out_shape=(out, out),
        in_specs=[in_vmem] * 5,
        out_specs=(anywhere, anywhere),
        scratch_shapes=[pltpu.VMEM(second.shape, second.dtype), pltpu.SemaphoreType.DMA((7,))],
        name="last",
        compiler_params=pltpu.CompilerParams(vmem_limit_bytes=16 * 1024 * 1024),
        cost_estimate=pl.CostEstimate(flops=WEIGHT << 26, bytes_accessed=5 * second.size, transcendentals=0),
    )(sums, state, came, flags, second)


def shifted(block, axis, distance):
    devices = range(lax.axis_size(axis))
    route = [(i - distance, i) for i in devices if i - distance in devices]
    return lax.ppermute(block, axis, route)


def stays(below, above):
    section, size = lax.axis_index("section"), lax.axis_size("section")
    here = jnp.where(section == size - 1, below, above)
    if size > 2:
        here = jnp.where((section == size - 1) | (section == 0), here, shifted(below, "section", 1))
    return here


def crosses(below, above):
    section, size = lax.axis_index("section"), lax.axis_size("section")
    if size == 2:
        return lax.ppermute(jnp.where(section == size - 1, above, below), "section", [(0, 1), (1, 0)])
    return jnp.where(section == size - 1, shifted(below, "section", 1), shifted(above, "section", -1))


def after(x, *others):
    return lax.optimization_barrier((x, *others))[0]


def on_device(down_queries, down_keys, down_values, up_queries, up_keys, up_values, key_blocks):
    spacing = lax.axis_size("ctx") // 4
    onward = lambda x: shifted(x, "ctx", -spacing)
    back = lambda x: shifted(x, "ctx", spacing)
    pairs = tuple((d[0], u[0]) for d, u in ((down_queries, up_queries), (down_keys, up_keys), (down_values, up_values)))
    count = down_queries.shape[2] // TILE
    half = count // 2
    spread_flags = lambda x: jnp.broadcast_to(jnp.where(x >= 0, 1.0, 0.0).astype(jnp.float32).reshape(2, 1), (2, TILE))

    key, value = stays(*pairs[1]), stays(*pairs[2])
    far = back(jnp.concatenate([key, value], 0))
    query2 = crosses(*pairs[0])
    query = stays(*pairs[0])
    key2, value2 = crosses(*pairs[1]), crosses(*pairs[2])
    once_a = onward(query2[:, : half * TILE])
    once_b = onward(query2[:, half * TILE :])
    twice_a = onward(once_a)
    twice_b = onward(after(once_b, once_a))
    flags = spread_flags(key_blocks)
    next_blocks = onward(key_blocks)

    far_a = attend(FAR, half, 0, twice_a, key2, value2)
    back_a = back(far_a)
    once = onward(after(query, far_a))
    far_b = attend(FAR, count - half, half, after(twice_b, far_a, far), key2, value2)
    back_b = back(far_b)
    next_flags = spread_flags(after(next_blocks, far_b))
    near_a = attend(NEAR, half, 0, once_a, key2, value2, after(back_a, far_b), next_flags)
    done_a = back(near_a)
    near_b = attend(NEAR, count - half, half, once_b, key2, value2, after(back_b, near_a), next_flags)
    done_b = back(near_b)
    near = attend(BOTH, count, 0, after(once, near_b), key, value, far, next_flags)
    done = back(near)
    out2 = attend(OWN, half, 0, query2, key2, value2, after(done_a, near), flags)
    out2 = attend(OWN, count - half, half, query2, key2, value2, done_b, flags, out2)
    sums, state = attend(LOCAL, count, 0, after(query, out2), key, value)
    return finish(sums, state, after(done, sums), flags, out2)


def solution(mesh):
    placed = (P("section", "ctx", None),) * 6 + (P("ctx", None),)
    return jax.shard_map(
        on_device,
        mesh=mesh,
        in_specs=placed,
        out_specs=(P("section", "ctx", None), P("section", "ctx", None)),
        check_vma=False,
    )
```
